32 devices in a mesh: groups: 2 (over x), lon: 16 (over z, y, core).
Axes of the slice: x: 2, y: 2, z: 4, core: 2. Of those that a mesh axis runs over, the one named last changes fastest.
Arguments:
- column_state: float32 [2, 32, 2048, 2, 128], P('groups', None, 'lon'), parts along dimension 0, may hold values from -6 to 6
- daylit: int32 [2, 32, 2048], P('groups', None, 'lon'), parts along dimension 0, may hold values from 0 to 1, as said below
- courant_lon: float32 [2, 32, 2048], P('groups', None, 'lon'), parts along dimension 0, may hold values from -0.4 to 0.4
- courant_lat: float32 [2, 32, 2048], P('groups', None, 'lon'), parts along dimension 0, may hold values from -0.4 to 0.4
- w_in: bfloat16 [256, 512], replicated, may hold values from -0.5 to 0.5
- w_mid_a: bfloat16 [512, 512], replicated, may hold values from -0.375 to 0.375
- w_mid_b: bfloat16 [512, 512], replicated, may hold values from -0.375 to 0.375
- w_out: bfloat16 [512, 128], replicated, may hold values from -0.375 to 0.375
Outputs:
- new_state: float32 [2, 32, 2048, 2, 128], P('groups', None, 'lon'), parts along dimension 0
The draws below stay inside these ranges and needn't reach their ends.
There are 2 independent parts, one for each index of `groups`. The reference program is written for one: setup_inputs(seed, part) draws one part's arguments, and reference() takes and returns one part's arrays. A program takes and returns all parts, laid end to end along the dimension named above; an argument that names none is the same for every part. Nothing has to cross between parts.
Inputs may be any that keep to these rules, and one draw needn't show every extreme that they name: In every member and latitude row the daylit columns form one cyclic run of 1024 longitudes, so of the columns at longitudes g and g + 1024 exactly one is daylit.
All inputs are finite; a program needn't handle non-finite values.
Results may differ from the reference program's by a relative error of at most 0.005.
Values may be sent and summed in bfloat16 or wider, within the bound.
A program may use at most 64 MiB of HBM per device.

```python
import jax
import jax.numpy as jnp
from jax import lax

MEMBERS = 1
LEV = 128
HID = 512
FEAT = 256
LAT = 32
LON_DEV = 128
LONT = 2048


def draw_daylit(key, part):
    key = jax.random.fold_in(key, 7)
    key_sun, key_tilt = jax.random.split(key)
    sun_column = jax.random.randint(key_sun, (MEMBERS, 1, 1), 0, LONT)
    tilt_rows = jax.random.randint(key_tilt, (MEMBERS, LAT, 1), 0, 3 * LON_DEV)
    longitude = jnp.arange(LONT, dtype=jnp.int32)
    phase_cells = (longitude[None, None, :] + tilt_rows - sun_column) % LONT
    return (phase_cells < LONT // 2).astype(jnp.int32)


def level_of(rng, dims, shards, smallest, high):
    def one(dim, blocks):
        draws = jax.random.uniform(jax.random.fold_in(jax.random.fold_in(rng, 6), dim), (blocks,), jnp.float32, smallest / len(shards), high / len(shards))
        return jnp.repeat(jnp.exp(draws), dims[dim] // blocks).reshape((-1,) + (1,) * (len(dims) - dim - 1))

    loudness = one(*shards[0])
    for cut in shards[1:]:
        loudness = loudness * one(*cut)
    return loudness


def bell_draw(stream_key, extent, width, bound, pieces=(), held_as=jnp.bfloat16):
    drawn = width * jax.random.normal(stream_key, extent, jnp.float32)
    if pieces:
        drawn = drawn * level_of(stream_key, extent, pieces, -0.22, 0.18)
    return jnp.clip(drawn, -bound, bound).astype(held_as)


def setup_inputs(seed: int = 0, part: int = 0) -> dict:
    splits = jax.random.split(jax.random.key(seed), 9)
    part_keys = jax.random.split(jax.random.fold_in(splits[8], part), 9)
    return {
        "column_state": bell_draw(part_keys[0], (MEMBERS, LAT, LONT, 2, LEV), 1.0, 6.0, ((2, 16),), jnp.float32),
        "daylit": draw_daylit(jax.random.fold_in(jax.random.fold_in(splits[8], part), 71), part),
        "courant_lon": jnp.clip(jax.random.uniform(part_keys[2], (MEMBERS, LAT, LONT), jnp.float32, -0.4, 0.4) * level_of(part_keys[2], (MEMBERS, LAT, LONT), ((2, 16),), -0.4, 0.0), -0.4, 0.4),
        "courant_lat": jnp.clip(jax.random.uniform(part_keys[3], (MEMBERS, LAT, LONT), jnp.float32, -0.4, 0.4) * level_of(part_keys[3], (MEMBERS, LAT, LONT), ((2, 16),), -0.4, 0.0), -0.4, 0.4),
        "w_in": bell_draw(splits[4], (FEAT, HID), (4 * FEAT // 9) ** -0.5, 0.5),
        "w_mid_a": bell_draw(splits[5], (HID, HID), (4 * HID // 9) ** -0.5, 0.375),
        "w_mid_b": bell_draw(splits[6], (HID, HID), (4 * HID // 9) ** -0.5, 0.375),
        "w_out": bell_draw(splits[7], (HID, LEV), (4 * HID // 9) ** -0.5, 0.375),
    }


def radiate(rows, w_in, w_mid_a, w_mid_b, w_out):
    hidden = jax.nn.silu(jnp.dot(rows, w_in, preferred_element_type=jnp.float32)).astype(jnp.bfloat16)
    hidden = jax.nn.silu(jnp.dot(hidden, w_mid_a, preferred_element_type=jnp.float32)).astype(jnp.bfloat16)
    hidden = jax.nn.silu(jnp.dot(hidden, w_mid_b, preferred_element_type=jnp.float32)).astype(jnp.bfloat16)
    return jnp.dot(hidden, w_out, preferred_element_type=jnp.float32).astype(jnp.bfloat16)


def member_step(column_state, daylit, courant_lon, courant_lat, w_in, w_mid_a, w_mid_b, w_out):
    inputs = column_state.astype(jnp.bfloat16).reshape(LAT, LONT, FEAT)
    rates = lax.map(lambda row_inputs: radiate(row_inputs, w_in, w_mid_a, w_mid_b, w_out), inputs)
    heat_rates = jnp.where(daylit[:, :, None] == 1, rates, jnp.zeros_like(rates))
    east_cells = jnp.roll(column_state, -1, axis=1)
    west_cells = jnp.roll(column_state, 1, axis=1)
    lat_padded = jnp.pad(column_state, ((1, 1), (0, 0), (0, 0), (0, 0)))
    north_cells = lat_padded[2:]
    south_cells = lat_padded[:-2]
    push_lon = courant_lon[:, :, None, None]
    push_lat = courant_lat[:, :, None, None]
    tendency = (-push_lon * (east_cells - west_cells) * 0.5 - push_lat * (north_cells - south_cells) * 0.5
                + 0.1 * (east_cells + west_cells + north_cells + south_cells - 4.0 * column_state))
    heat_field = heat_rates.astype(jnp.float32)
    heating = jnp.stack([heat_field, jnp.zeros_like(heat_field)], axis=2)
    return column_state + tendency + heating


def reference(column_state, daylit, courant_lon, courant_lat, w_in, w_mid_a, w_mid_b, w_out):
    results = []
    for member in range(MEMBERS):
        results.append(member_step(column_state[member], daylit[member], courant_lon[member],
                                   courant_lat[member], w_in, w_mid_a, w_mid_b, w_out))
    return jnp.stack(results, axis=0)
```

```python
import functools

import jax
import jax.numpy as jnp
from jax import lax
from jax.experimental import pallas as pl
from jax.experimental.pallas import tpu as pltpu
from jax.sharding import PartitionSpec as P

PAD = 8


def silu_half(half):
    return half + half * jnp.tanh(half)


def column_kernel(chunk, x_hbm, coef_hbm, low_hbm, high_hbm, w_in_hbm, w_a_hbm, w_b_hbm, w_out_hbm,
                  out_hbm, xs, outs, coef, low, high, turned, w_in, w_a, w_b, w_out,
                  x_sems, w_sems, out_sems):
    lat, width, lev = x_hbm.shape
    cols = width // 2
    steps = lat // chunk

    def x_copy(i):
        return pltpu.make_async_copy(
            x_hbm.at[pl.ds(i * chunk, chunk)],
            xs.at[pl.ds(1 + i * chunk, chunk), pl.ds(PAD, width)],
            x_sems.at[i],
        )

    def out_copy(i):
        return pltpu.make_async_copy(
            outs.at[pl.ds(i * chunk, chunk)], out_hbm.at[pl.ds(i * chunk, chunk)], out_sems.at[i]
        )

    smalls = [
        pltpu.make_async_copy(source, target, w_sems.at[k])
        for k, (source, target) in enumerate([
            (w_in_hbm, w_in), (w_a_hbm, w_a), (w_b_hbm, w_b), (w_out_hbm, w_out),
            (coef_hbm, coef), (low_hbm, low), (high_hbm, high),
        ])
    ]
    x_copy(0).start()
    for copy in smalls:
        copy.start()

    @pl.loop(1, steps)
    def _(i):
        x_copy(i).start()

    blank = jnp.zeros((width, lev), jnp.float32)
    xs[0, pl.ds(PAD, width)] = blank
    xs[lat + 1, pl.ds(PAD, width)] = blank
    for copy in smalls:
        copy.wait()
    for w in (w_in, w_a, w_b):
        w[...] = w[...] * jnp.bfloat16(0.5)
    turned[...] = coef[...].T
    xs[pl.ds(1, lat), pl.ds(PAD - 2, 2)] = low[...].astype(jnp.float32)
    xs[pl.ds(1, lat), pl.ds(PAD + width, 2)] = high[...].astype(jnp.float32)
    x_copy(0).wait()

    def picked(r):
        at = jnp.full((cols, 128), r, jnp.int32)
        return jnp.take_along_axis(turned[...], at, axis=1, mode="promise_in_bounds")

    @pl.loop(0, steps)
    def _(i):
        @pl.when(i < steps - 1)
        def _():
            x_copy(i + 1).wait()

        first = i * chunk
        rows = []
        for q in range(chunk):
            rows.append(jnp.concatenate([
                xs[1 + first + q, pl.ds(PAD + f, cols, stride=2), :].astype(jnp.bfloat16)
                for f in range(2)
            ], axis=1))
        hidden = jnp.concatenate(rows, axis=0)
        for w in (w_in, w_a, w_b):
            hidden = silu_half(
                jnp.dot(hidden, w[...], preferred_element_type=jnp.float32)
            ).astype(jnp.bfloat16)
        rates = jnp.dot(hidden, w_out[...], preferred_element_type=jnp.float32)
        for q in range(chunk):
            r = first + q
            push_lon = picked(r)
            push_lat = picked(lat + r)
            lit = picked(2 * lat + r)
            heat = jnp.where(lit > 0.5, rates[q * cols:(q + 1) * cols], 0.0)
            for f in range(2):
                mid = xs[1 + r, pl.ds(PAD + f, cols, stride=2), :]
                east = xs[1 + r, pl.ds(PAD + 2 + f, cols, stride=2), :]
                west = xs[1 + r, pl.ds(PAD - 2 + f, cols, stride=2), :]
                north = xs[2 + r, pl.ds(PAD + f, cols, stride=2), :]
                south = xs[r, pl.ds(PAD + f, cols, stride=2), :]
                new = (0.6 * mid + 0.1 * ((east + west) + (north + south))
                       - push_lon * (east - west) - push_lat * (north - south))
                if f == 0:
                    new = new + heat
                outs[r, pl.ds(f, cols, stride=2), :] = new
        out_copy(i).start()

    @pl.loop(0, steps)
    def _(i):
        out_copy(i).wait()


def column_step(x, coef, low, high, w_in, w_a, w_b, w_out, chunk):
    lat, width, lev = x.shape
    steps = lat // chunk
    anywhere = pl.BlockSpec(memory_space=pl.ANY)
    return pl.pallas_call(
        functools.partial(column_kernel, chunk),
        out_shape=jax.ShapeDtypeStruct(x.shape, jnp.float32),
        in_specs=[anywhere] * 8,
        out_specs=anywhere,
        scratch_shapes=[
            pltpu.VMEM((lat + 2, width + 2 * PAD, lev), jnp.float32),
            pltpu.VMEM(x.shape, jnp.float32),
            pltpu.VMEM(coef.shape, jnp.float32),
            pltpu.VMEM(low.shape, low.dtype),
            pltpu.VMEM(high.shape, high.dtype),
            pltpu.VMEM(coef.shape[::-1], jnp.float32),
            pltpu.VMEM(w_in.shape, w_in.dtype),
            pltpu.VMEM(w_a.shape, w_a.dtype),
            pltpu.VMEM(w_b.shape, w_b.dtype),
            pltpu.VMEM(w_out.shape, w_out.dtype),
            pltpu.SemaphoreType.DMA((steps,)),
            pltpu.SemaphoreType.DMA((7,)),
            pltpu.SemaphoreType.DMA((steps,)),
        ],
        compiler_params=pltpu.CompilerParams(vmem_limit_bytes=48 * 1024 * 1024),
        cost_estimate=pl.CostEstimate(
            flops=2 * lat * width // 2 * 720896, bytes_accessed=10 * 1024 * 1024,
            transcendentals=lat * width // 2 * 1536,
        ),
        name="column_step",
    )(x, coef, low, high, w_in, w_a, w_b, w_out)


def shards(column_state, daylit, courant_lon, courant_lat, w_in, w_mid_a, w_mid_b, w_out):
    _, lat, cols, fields, lev = column_state.shape
    count = lax.axis_size("lon")
    state = column_state[0]
    up = [(i, (i + 1) % count) for i in range(count)]
    down = [(b, a) for a, b in up]
    low = lax.ppermute(state[:, cols - 1].astype(jnp.bfloat16), "lon", up)
    high = lax.ppermute(state[:, 0].astype(jnp.bfloat16), "lon", down)
    coef = jnp.concatenate([
        0.5 * courant_lon[0], 0.5 * courant_lat[0], daylit[0].astype(jnp.float32),
        jnp.zeros((128 - 3 * lat, cols), jnp.float32),
    ], axis=0)
    out = column_step(
        state.reshape(lat, cols * fields, lev), coef, low, high, w_in, w_mid_a, w_mid_b, w_out, 4
    )
    return out.reshape(column_state.shape)


def solution(mesh):
    placed = (
        P("groups", None, "lon", None, None),
        P("groups", None, "lon"),
        P("groups", None, "lon"),
        P("groups", None, "lon"),
        P(),
        P(),
        P(),
        P(),
    )
    return jax.shard_map(
        shards,
        mesh=mesh,
        in_specs=placed,
        out_specs=P("groups", None, "lon", None, None),
        check_vma=False,
    )
```

```python
import functools

import jax
import jax.numpy as jnp
from jax import lax
from jax.experimental import pallas as pl
from jax.experimental.pallas import tpu as pltpu
from jax.sharding import PartitionSpec as P

PAD = 8
EARLY_MIB = 58


def silu_half(half):
    return half + half * jnp.tanh(half)


def halved(*weights):
    for w in weights:
        w[...] = w[...] * jnp.bfloat16(0.5)


def network(hidden, weights, w_out):
    for w in weights:
        hidden = silu_half(
            jnp.dot(hidden, w[...], preferred_element_type=jnp.float32)
        ).astype(jnp.bfloat16)
    return jnp.dot(hidden, w_out[...], preferred_element_type=jnp.float32)


def early_kernel(chunk, early, x_hbm, w_in_hbm, w_a_hbm, w_b_hbm, w_out_hbm,
                 rates_ref, low_ref, high_ref,
                 xs, edges, packed, landed, w_in, w_a, w_b, w_out,
                 x_sems, w_sems, edge_sems, send_sems, recv_sems):
    lat, width, lev = x_hbm.shape
    cols = width // 2
    steps = early // chunk
    count = lax.axis_size("lon")
    me = lax.axis_index("lon")
    right = lax.rem(me + 1, count)
    left = lax.rem(me + count - 1, count)
    barrier = pltpu.get_barrier_semaphore()
    for other in (left, right):
        pl.semaphore_signal(
            barrier, inc=1, device_id={"lon": other}, device_id_type=pl.DeviceIdType.MESH
        )

    def x_copy(i):
        return pltpu.make_async_copy(
            x_hbm.at[pl.ds(i * chunk, chunk)], xs.at[pl.ds(i * chunk, chunk)], x_sems.at[i]
        )

    edge_copies = [
        pltpu.make_async_copy(
            x_hbm.at[:, pl.ds(start, PAD)], edges.at[side], edge_sems.at[side]
        )
        for side, start in enumerate((0, width - PAD))
    ]
    w_copies = [
        pltpu.make_async_copy(source, target, w_sems.at[k])
        for k, (source, target) in enumerate([
            (w_in_hbm, w_in), (w_a_hbm, w_a), (w_b_hbm, w_b), (w_out_hbm, w_out),
        ])
    ]
    w_copies[0].start()
    x_copy(0).start()
    for copy in w_copies[1:]:
        copy.start()
    for copy in edge_copies:
        copy.start()
    for i in range(1, steps):
        x_copy(i).start()

    sends = [
        pltpu.make_async_remote_copy(
            src_ref=packed.at[side], dst_ref=landed.at[side],
            send_sem=send_sems.at[side], recv_sem=recv_sems.at[side],
            device_id={"lon": other}, device_id_type=pl.DeviceIdType.MESH,
        )
        for side, other in enumerate((left, right))
    ]
    for copy in w_copies:
        copy.wait()
    halved(w_in, w_a, w_b)
    for side, copy in enumerate(edge_copies):
        copy.wait()
        for f in range(2):
            inner = f if side == 0 else PAD - 2 + f
            packed[side, pl.ds(f * lat, lat)] = edges[side, :, inner, :]

    @pl.loop(0, steps)
    def _(i):
        @pl.when(i == 1)
        def _():
            pl.semaphore_wait(barrier, 2)
            for send in sends:
                send.start()

        x_copy(i).wait()
        rows = [
            jnp.concatenate([
                xs[i * chunk + q, pl.ds(f, cols, stride=2), :].astype(jnp.bfloat16)
                for f in range(2)
            ], axis=1)
            for q in range(chunk)
        ]
        rates = network(jnp.concatenate(rows, axis=0), (w_in, w_a, w_b), w_out)
        rates_ref[pl.ds(i * chunk, chunk)] = rates.astype(jnp.bfloat16).reshape(chunk, cols, lev)

    for send in sends:
        send.wait()
    high_ref[...] = landed[0]
    low_ref[...] = landed[1]


def early_part(x, w_in, w_a, w_b, w_out, chunk, early):
    lat, width, lev = x.shape
    steps = early // chunk
    anywhere = pl.BlockSpec(memory_space=pl.ANY)
    kept = pl.BlockSpec(memory_space=pltpu.VMEM)
    halo = jax.ShapeDtypeStruct((2 * lat, lev), jnp.float32)
    return pl.pallas_call(
        functools.partial(early_kernel, chunk, early),
        out_shape=[jax.ShapeDtypeStruct((early, width // 2, lev), jnp.bfloat16), halo, halo],
        in_specs=[anywhere] * 5,
        out_specs=[kept] * 3,
        scratch_shapes=[
            pltpu.VMEM((early, width, lev), jnp.float32),
            pltpu.VMEM((2, lat, PAD, lev), jnp.float32),
            pltpu.VMEM((2, 2 * lat, lev), jnp.float32),
            pltpu.VMEM((2, 2 * lat, lev), jnp.float32),
            pltpu.VMEM(w_in.shape, w_in.dtype),
            pltpu.VMEM(w_a.shape, w_a.dtype),
            pltpu.VMEM(w_b.shape, w_b.dtype),
            pltpu.VMEM(w_out.shape, w_out.dtype),
            pltpu.SemaphoreType.DMA((steps,)),
            pltpu.SemaphoreType.DMA((4,)),
            pltpu.SemaphoreType.DMA((2,)),
            pltpu.SemaphoreType.DMA((2,)),
            pltpu.SemaphoreType.DMA((2,)),
        ],
        compiler_params=pltpu.CompilerParams(
            vmem_limit_bytes=EARLY_MIB * 1024 * 1024, collective_id=0, has_side_effects=True
        ),
        cost_estimate=pl.CostEstimate(
            flops=early * width * 720896, bytes_accessed=4 * 1024 * 1024,
            transcendentals=early * width // 2 * 1536,
        ),
        name="early_part",
    )(x, w_in, w_a, w_b, w_out)


def column_kernel(chunk, early, x_hbm, lit_hbm, lon_hbm, lat_hbm, rates_hbm, low_hbm, high_hbm,
                  w_in_hbm, w_a_hbm, w_b_hbm, w_out_hbm,
                  out_hbm, xs, outs, coef, lit, early_rates, low, high, turned,
                  w_in, w_a, w_b, w_out, x_sems, w_sems, out_sems):
    lat, width, lev = x_hbm.shape
    cols = width // 2
    steps = lat // chunk
    ready = early // chunk

    def x_copy(i):
        return pltpu.make_async_copy(
            x_hbm.at[pl.ds(i * chunk, chunk)],
            xs.at[pl.ds(1 + i * chunk, chunk), pl.ds(PAD, width)],
            x_sems.at[i],
        )

    def out_copy(i):
        return pltpu.make_async_copy(
            outs.at[pl.ds(i * chunk, chunk)], out_hbm.at[pl.ds(i * chunk, chunk)], out_sems.at[i]
        )

    smalls = [
        pltpu.make_async_copy(source, target, w_sems.at[k])
        for k, (source, target) in enumerate([
            (low_hbm, low), (high_hbm, high), (lon_hbm, coef.at[pl.ds(0, lat)]),
            (lat_hbm, coef.at[pl.ds(lat, lat)]), (lit_hbm, lit),
            (w_in_hbm, w_in), (w_a_hbm, w_a), (w_b_hbm, w_b), (w_out_hbm, w_out),
            (rates_hbm, early_rates),
        ])
    ]
    x_copy(ready).start()
    for copy in smalls:
        copy.start()
    for i in (0, ready - 1):
        x_copy(i).start()
    for i in range(1, ready):
        x_copy(ready + i).start()
        if i < ready - 1:
            x_copy(i).start()

    blank = jnp.zeros((width, lev), jnp.float32)
    xs[0, pl.ds(PAD, width)] = blank
    xs[lat + 1, pl.ds(PAD, width)] = blank
    for copy in smalls:
        copy.wait()
    halved(w_in, w_a, w_b)
    half = 0.5 * coef[pl.ds(0, 2 * lat)]
    turned[...] = jnp.concatenate([
        half, lit[...].astype(jnp.float32), jnp.zeros((128 - 3 * lat, cols), jnp.float32)
    ], axis=0).T
    for r in range(lat):
        for f in range(2):
            xs[1 + r, pl.ds(PAD - 2 + f, 1)] = low[pl.ds(f * lat + r, 1)]
            xs[1 + r, pl.ds(PAD + width + f, 1)] = high[pl.ds(f * lat + r, 1)]
    for i in (ready, 0, ready - 1):
        x_copy(i).wait()

    def picked(r):
        at = jnp.full((cols, 128), r, jnp.int32)
        return jnp.take_along_axis(turned[...], at, axis=1, mode="promise_in_bounds")

    def move(first, rates):
        for q in range(chunk):
            r = first + q
            push_lon = picked(r)
            push_lat = picked(lat + r)
            lit_here = picked(2 * lat + r)
            heat = jnp.where(lit_here > 0.5, rates(q), 0.0)
            for f in range(2):
                mid = xs[1 + r, pl.ds(PAD + f, cols, stride=2), :]
                east = xs[1 + r, pl.ds(PAD + 2 + f, cols, stride=2), :]
                west = xs[1 + r, pl.ds(PAD - 2 + f, cols, stride=2), :]
                north = xs[2 + r, pl.ds(PAD + f, cols, stride=2), :]
                south = xs[r, pl.ds(PAD + f, cols, stride=2), :]
                new = (0.6 * mid + 0.1 * ((east + west) + (north + south))
                       - push_lon * (east - west) - push_lat * (north - south))
                if f == 0:
                    new = new + heat
                outs[r, pl.ds(f, cols, stride=2), :] = new

    def late_rates(first):
        rows = []
        for q in range(chunk):
            rows.append(jnp.concatenate([
                xs[1 + first + q, pl.ds(PAD + f, cols, stride=2), :].astype(jnp.bfloat16)
                for f in range(2)
            ], axis=1))
        return network(jnp.concatenate(rows, axis=0), (w_in, w_a, w_b), w_out)

    @pl.loop(0, ready)
    def _(i):
        @pl.when(i < ready - 1)
        def _():
            x_copy(i + 1 + ready).wait()

        @pl.when(i < ready - 2)
        def _():
            x_copy(i + 1).wait()

        late = (i + ready) * chunk
        rates = late_rates(late)
        soon = i * chunk
        move(soon, lambda q: early_rates[soon + q].astype(jnp.float32))
        out_copy(i).start()
        move(late, lambda q: rates[q * cols:(q + 1) * cols])
        out_copy(i + ready).start()

    @pl.loop(0, steps)
    def _(i):
        out_copy(i).wait()


def column_step(x, lit, lon, lat_push, rates, low, high, w_in, w_a, w_b, w_out, chunk, early):
    lat, width, lev = x.shape
    steps = lat // chunk
    anywhere = pl.BlockSpec(memory_space=pl.ANY)
    return pl.pallas_call(
        functools.partial(column_kernel, chunk, early),
        out_shape=jax.ShapeDtypeStruct(x.shape, jnp.float32),
        in_specs=[anywhere] * 11,
        out_specs=anywhere,
        scratch_shapes=[
            pltpu.VMEM((lat + 2, width + 2 * PAD, lev), jnp.float32),
            pltpu.VMEM(x.shape, jnp.float32),
            pltpu.VMEM((2 * lat, width // 2), jnp.float32),
            pltpu.VMEM(lit.shape, lit.dtype),
            pltpu.VMEM(rates.shape, rates.dtype),
            pltpu.VMEM(low.shape, low.dtype),
            pltpu.VMEM(high.shape, high.dtype),
            pltpu.VMEM((width // 2, 128), jnp.float32),
            pltpu.VMEM(w_in.shape, w_in.dtype),
            pltpu.VMEM(w_a.shape, w_a.dtype),
            pltpu.VMEM(w_b.shape, w_b.dtype),
            pltpu.VMEM(w_out.shape, w_out.dtype),
            pltpu.SemaphoreType.DMA((steps,)),
            pltpu.SemaphoreType.DMA((10,)),
            pltpu.SemaphoreType.DMA((steps,)),
        ],
        compiler_params=pltpu.CompilerParams(vmem_limit_bytes=56 * 1024 * 1024),
        cost_estimate=pl.CostEstimate(
            flops=(lat - early) * width * 720896, bytes_accessed=10 * 1024 * 1024,
            transcendentals=(lat - early) * width // 2 * 1536,
        ),
        name="column_step",
    )(x, lit, lon, lat_push, rates, low, high, w_in, w_a, w_b, w_out)


def shards(column_state, daylit, courant_lon, courant_lat, w_in, w_mid_a, w_mid_b, w_out):
    _, lat, cols, fields, lev = column_state.shape
    x = column_state.reshape(lat, cols * fields, lev)
    weights = (w_in, w_mid_a, w_mid_b, w_out)
    chunk, early = 4, lat // 2
    rates, low, high = early_part(x, *weights, chunk, early)
    out = column_step(
        x, daylit[0], courant_lon[0], courant_lat[0], rates, low, high, *weights, chunk, early
    )
    return out.reshape(column_state.shape)


def solution(mesh):
    placed = (
        P("groups", None, "lon", None, None),
        P("groups", None, "lon"),
        P("groups", None, "lon"),
        P("groups", None, "lon"),
        P(),
        P(),
        P(),
        P(),
    )
    return jax.shard_map(
        shards,
        mesh=mesh,
        in_specs=placed,
        out_specs=P("groups", None, "lon", None, None),
        check_vma=False,
    )
```

```python
import functools

import jax
import jax.numpy as jnp
from jax import lax
from jax.experimental import pallas as pl
from jax.experimental.pallas import tpu as pltpu
from jax.sharding import PartitionSpec as P

PAD = 8
KERNEL_MIB = 46


def silu_half(half):
    return half + half * jnp.tanh(half)


def halved(*weights):
    for w in weights:
        w[...] = w[...] * jnp.bfloat16(0.5)


def network(hidden, weights, w_out):
    for w in weights:
        hidden = silu_half(
            jnp.dot(hidden, w[...], preferred_element_type=jnp.float32)
        ).astype(jnp.bfloat16)
    return jnp.dot(hidden, w_out[...], preferred_element_type=jnp.float32)


def column_kernel(chunk, x_hbm, lit_hbm, lon_hbm, lat_hbm, w_in_hbm, w_a_hbm, w_b_hbm, w_out_hbm,
                  outs, xs, edges, packed, landed, coef, lit, turned, w_in, w_a, w_b, w_out,
                  x_sems, w_sems, edge_sems, send_sems, recv_sems):
    lat, width, lev = x_hbm.shape
    cols = width // 2
    steps = lat // chunk
    count = lax.axis_size("lon")
    me = lax.axis_index("lon")
    right = lax.rem(me + 1, count)
    left = lax.rem(me + count - 1, count)
    barrier = pltpu.get_barrier_semaphore()
    for other in (left, right):
        pl.semaphore_signal(
            barrier, inc=1, device_id={"lon": other}, device_id_type=pl.DeviceIdType.MESH
        )

    def x_copy(i):
        return pltpu.make_async_copy(
            x_hbm.at[pl.ds(i * chunk, chunk)],
            xs.at[pl.ds(1 + i * chunk, chunk), pl.ds(PAD, width)],
            x_sems.at[i],
        )

    edge_copies = [
        pltpu.make_async_copy(
            x_hbm.at[:, pl.ds(start, PAD)], edges.at[side], edge_sems.at[side]
        )
        for side, start in enumerate((0, width - PAD))
    ]
    smalls = [
        pltpu.make_async_copy(source, target, w_sems.at[k])
        for k, (source, target) in enumerate([
            (w_in_hbm, w_in), (lon_hbm, coef.at[pl.ds(0, lat)]),
            (lat_hbm, coef.at[pl.ds(lat, lat)]), (lit_hbm, lit),
            (w_a_hbm, w_a), (w_b_hbm, w_b), (w_out_hbm, w_out),
        ])
    ]
    for copy in edge_copies:
        copy.start()
    x_copy(0).start()
    for copy in smalls:
        copy.start()
    for i in range(1, steps):
        x_copy(i).start()

    sends = [
        pltpu.make_async_remote_copy(
            src_ref=packed.at[side], dst_ref=landed.at[side],
            send_sem=send_sems.at[side], recv_sem=recv_sems.at[side],
            device_id={"lon": other}, device_id_type=pl.DeviceIdType.MESH,
        )
        for side, other in enumerate((left, right))
    ]
    blank = jnp.zeros((width, lev), jnp.float32)
    xs[0, pl.ds(PAD, width)] = blank
    xs[lat + 1, pl.ds(PAD, width)] = blank
    nothing = jnp.zeros((lat, PAD, lev), jnp.float32)
    xs[pl.ds(1, lat), pl.ds(0, PAD)] = nothing
    xs[pl.ds(1, lat), pl.ds(PAD + width, PAD)] = nothing
    for side, copy in enumerate(edge_copies):
        copy.wait()
        for f in range(2):
            inner = f if side == 0 else PAD - 2 + f
            packed[side, pl.ds(f * lat, lat)] = edges[side, :, inner, :]
    for copy in smalls:
        copy.wait()
    halved(w_in, w_a, w_b)
    half = 0.5 * coef[...]
    turned[...] = jnp.concatenate([
        half, lit[...].astype(jnp.float32), jnp.zeros((128 - 3 * lat, cols), jnp.float32)
    ], axis=0).T
    x_copy(0).wait()

    def picked(r):
        at = jnp.full((cols, 128), r, jnp.int32)
        return jnp.take_along_axis(turned[...], at, axis=1, mode="promise_in_bounds")

    @pl.loop(0, steps)
    def _(i):
        @pl.when(i == 1)
        def _():
            pl.semaphore_wait(barrier, 2)
            for send in sends:
                send.start()

        @pl.when(i < steps - 1)
        def _():
            x_copy(i + 1).wait()

        first = i * chunk
        rows = [
            jnp.concatenate([
                xs[1 + first + q, pl.ds(PAD + f, cols, stride=2), :].astype(jnp.bfloat16)
                for f in range(2)
            ], axis=1)
            for q in range(chunk)
        ]
        rates = network(jnp.concatenate(rows, axis=0), (w_in, w_a, w_b), w_out)
        for q in range(chunk):
            r = first + q
            push_lon = picked(r)
            push_lat = picked(lat + r)
            lit_here = picked(2 * lat + r)
            heat = jnp.where(lit_here > 0.5, rates[q * cols:(q + 1) * cols], 0.0)
            for f in range(2):
                mid = xs[1 + r, pl.ds(PAD + f, cols, stride=2), :]
                east = xs[1 + r, pl.ds(PAD + 2 + f, cols, stride=2), :]
                west = xs[1 + r, pl.ds(PAD - 2 + f, cols, stride=2), :]
                north = xs[2 + r, pl.ds(PAD + f, cols, stride=2), :]
                south = xs[r, pl.ds(PAD + f, cols, stride=2), :]
                new = (0.6 * mid + 0.1 * ((east + west) + (north + south))
                       - push_lon * (east - west) - push_lat * (north - south))
                if f == 0:
                    new = new + heat
                outs[r, pl.ds(f, cols, stride=2), :] = new

    for send in sends:
        send.wait()
    from_west = 0.1 + 0.5 * coef[pl.ds(0, lat), 0:1]
    from_east = 0.1 - 0.5 * coef[pl.ds(0, lat), cols - 1:cols]
    for f in range(2):
        field = pl.ds(f * lat, lat)
        outs[:, f, :] = outs[:, f, :] + from_west * landed[1, field]
        outs[:, width - 2 + f, :] = outs[:, width - 2 + f, :] + from_east * landed[0, field]


def column_step(x, lit, lon, lat_push, w_in, w_a, w_b, w_out, chunk):
    lat, width, lev = x.shape
    steps = lat // chunk
    anywhere = pl.BlockSpec(memory_space=pl.ANY)
    return pl.pallas_call(
        functools.partial(column_kernel, chunk),
        out_shape=jax.ShapeDtypeStruct(x.shape, jnp.float32),
        in_specs=[anywhere] * 8,
        out_specs=pl.BlockSpec(memory_space=pltpu.VMEM),
        scratch_shapes=[
            pltpu.VMEM((lat + 2, width + 2 * PAD, lev), jnp.float32),
            pltpu.VMEM((2, lat, PAD, lev), jnp.float32),
            pltpu.VMEM((2, 2 * lat, lev), jnp.float32),
            pltpu.VMEM((2, 2 * lat, lev), jnp.float32),
            pltpu.VMEM((2 * lat, width // 2), jnp.float32),
            pltpu.VMEM(lit.shape, lit.dtype),
            pltpu.VMEM((width // 2, 128), jnp.float32),
            pltpu.VMEM(w_in.shape, w_in.dtype),
            pltpu.VMEM(w_a.shape, w_a.dtype),
            pltpu.VMEM(w_b.shape, w_b.dtype),
            pltpu.VMEM(w_out.shape, w_out.dtype),
            pltpu.SemaphoreType.DMA((steps,)),
            pltpu.SemaphoreType.DMA((7,)),
            pltpu.SemaphoreType.DMA((2,)),
            pltpu.SemaphoreType.DMA((2,)),
            pltpu.SemaphoreType.DMA((2,)),
        ],
        compiler_params=pltpu.CompilerParams(
            vmem_limit_bytes=KERNEL_MIB * 1024 * 1024, collective_id=0, has_side_effects=True
        ),
        cost_estimate=pl.CostEstimate(
            flops=lat * width * 720896, bytes_accessed=10 * 1024 * 1024,
            transcendentals=lat * width // 2 * 1536,
        ),
        name="column_step",
    )(x, lit, lon, lat_push, w_in, w_a, w_b, w_out)


def shards(column_state, daylit, courant_lon, courant_lat, w_in, w_mid_a, w_mid_b, w_out):
    _, lat, cols, fields, lev = column_state.shape
    out = column_step(
        column_state.reshape(lat, cols * fields, lev), daylit[0], courant_lon[0], courant_lat[0],
        w_in, w_mid_a, w_mid_b, w_out, 4
    )
    return out.reshape(column_state.shape)


def solution(mesh):
    placed = (
        P("groups", None, "lon", None, None),
        P("groups", None, "lon"),
        P("groups", None, "lon"),
        P("groups", None, "lon"),
        P(),
        P(),
        P(),
        P(),
    )
    return jax.shard_map(
        shards,
        mesh=mesh,
        in_specs=placed,
        out_specs=P("groups", None, "lon", None, None),
        check_vma=False,
    )
```

```python
import functools

import jax
import jax.numpy as jnp
from jax import lax
from jax.experimental import pallas as pl
from jax.experimental.pallas import tpu as pltpu
from jax.sharding import PartitionSpec as P

PAD = 8
KERNEL_MIB = 46


def silu_half(half):
    return half + half * jnp.tanh(half)


def halved(*weights):
    for w in weights:
        w[...] = w[...] * jnp.bfloat16(0.5)


def network(hidden, weights, w_out):
    for w in weights:
        hidden = silu_half(
            jnp.dot(hidden, w[...], preferred_element_type=jnp.float32)
        ).astype(jnp.bfloat16)
    return jnp.dot(hidden, w_out[...], preferred_element_type=jnp.float32)


def column_kernel(chunk, x_hbm, lit_hbm, lon_hbm, lat_hbm, w_in_hbm, w_a_hbm, w_b_hbm, w_out_hbm,
                  outs, xs, edges, packed, landed, coef, lit, turned, w_in, w_a, w_b, w_out,
                  x_sems, w_sems, edge_sems, send_sems, recv_sems):
    lat, width, lev = x_hbm.shape
    cols = width // 2
    steps = lat // chunk
    count = lax.axis_size("lon")
    me = lax.axis_index("lon")
    right = lax.rem(me + 1, count)
    left = lax.rem(me + count - 1, count)
    barrier = pltpu.get_barrier_semaphore()
    for other in (left, right):
        pl.semaphore_signal(
            barrier, inc=1, device_id={"lon": other}, device_id_type=pl.DeviceIdType.MESH
        )

    def x_copy(i):
        return pltpu.make_async_copy(
            x_hbm.at[pl.ds(i * chunk, chunk)],
            xs.at[pl.ds(1 + i * chunk, chunk), pl.ds(PAD, width)],
            x_sems.at[i],
        )

    edge_copies = [
        pltpu.make_async_copy(
            x_hbm.at[:, pl.ds(start, PAD)], edges.at[side], edge_sems.at[side]
        )
        for side, start in enumerate((0, width - PAD))
    ]
    smalls = [
        pltpu.make_async_copy(source, target, w_sems.at[k])
        for k, (source, target) in enumerate([
            (w_in_hbm, w_in), (lon_hbm, coef.at[pl.ds(0, lat)]),
            (lat_hbm, coef.at[pl.ds(lat, lat)]), (lit_hbm, lit),
            (w_a_hbm, w_a), (w_b_hbm, w_b), (w_out_hbm, w_out),
        ])
    ]
    for copy in edge_copies:
        copy.start()
    x_copy(0).start()
    for copy in smalls:
        copy.start()
    for i in range(1, steps):
        x_copy(i).start()

    sends = [
        pltpu.make_async_remote_copy(
            src_ref=packed.at[side], dst_ref=landed.at[side],
            send_sem=send_sems.at[side], recv_sem=recv_sems.at[side],
            device_id={"lon": other}, device_id_type=pl.DeviceIdType.MESH,
        )
        for side, other in enumerate((left, right))
    ]
    blank = jnp.zeros((width, lev), jnp.float32)
    xs[0, pl.ds(PAD, width)] = blank
    xs[lat + 1, pl.ds(PAD, width)] = blank
    nothing = jnp.zeros((lat, PAD, lev), jnp.float32)
    xs[pl.ds(1, lat), pl.ds(0, PAD)] = nothing
    xs[pl.ds(1, lat), pl.ds(PAD + width, PAD)] = nothing
    for side, copy in enumerate(edge_copies):
        copy.wait()
        for f in range(2):
            inner = f if side == 0 else PAD - 2 + f
            packed[side, pl.ds(f * lat, lat)] = edges[side, :, inner, :]
    for copy in smalls:
        copy.wait()
    halved(w_in, w_a, w_b)
    half = 0.5 * coef[...]
    turned[...] = jnp.concatenate([
        half, lit[...].astype(jnp.float32), jnp.zeros((128 - 3 * lat, cols), jnp.float32)
    ], axis=0).T
    x_copy(0).wait()

    def picked(r):
        at = jnp.full((cols, 128), r, jnp.int32)
        return jnp.take_along_axis(turned[...], at, axis=1, mode="promise_in_bounds")

    @pl.loop(0, steps)
    def _(i):
        @pl.when(i == 1)
        def _():
            pl.semaphore_wait(barrier, 2)
            for send in sends:
                send.start()

        @pl.when(i < steps - 1)
        def _():
            x_copy(i + 1).wait()

        first = i * chunk
        rows = [
            jnp.concatenate([
                xs[1 + first + q, pl.ds(PAD + f, cols, stride=2), :].astype(jnp.bfloat16)
                for f in range(2)
            ], axis=1)
            for q in range(chunk)
        ]
        rates = network(jnp.concatenate(rows, axis=0), (w_in, w_a, w_b), w_out)
        for q in range(chunk):
            r = first + q
            push_lon = picked(r)
            push_lat = picked(lat + r)
            lit_here = picked(2 * lat + r)
            heat = jnp.where(lit_here > 0.5, rates[q * cols:(q + 1) * cols], 0.0)
            for f in range(2):
                mid = xs[1 + r, pl.ds(PAD + f, cols, stride=2), :]
                east = xs[1 + r, pl.ds(PAD + 2 + f, cols, stride=2), :]
                west = xs[1 + r, pl.ds(PAD - 2 + f, cols, stride=2), :]
                north = xs[2 + r, pl.ds(PAD + f, cols, stride=2), :]
                south = xs[r, pl.ds(PAD + f, cols, stride=2), :]
                new = (0.6 * mid + 0.1 * ((east + west) + (north + south))
                       - push_lon * (east - west) - push_lat * (north - south))
                if f == 0:
                    new = new + heat
                outs[r, pl.ds(f, cols, stride=2), :] = new

    for send in sends:
        send.wait()
    from_west = 0.1 + 0.5 * coef[pl.ds(0, lat), 0:1]
    from_east = 0.1 - 0.5 * coef[pl.ds(0, lat), cols - 1:cols]
    for f in range(2):
        field = pl.ds(f * lat, lat)
        outs[:, f, :] = outs[:, f, :] + from_west * landed[1, field]
        outs[:, width - 2 + f, :] = outs[:, width - 2 + f, :] + from_east * landed[0, field]


def column_step(x, lit, lon, lat_push, w_in, w_a, w_b, w_out, chunk):
    lat, width, lev = x.shape
    steps = lat // chunk
    anywhere = pl.BlockSpec(memory_space=pltpu.HBM)
    return pl.pallas_call(
        functools.partial(column_kernel, chunk),
        out_shape=jax.ShapeDtypeStruct(x.shape, jnp.float32),
        in_specs=[anywhere] * 8,
        out_specs=pl.BlockSpec(memory_space=pltpu.VMEM),
        scratch_shapes=[
            pltpu.VMEM((lat + 2, width + 2 * PAD, lev), jnp.float32),
            pltpu.VMEM((2, lat, PAD, lev), jnp.float32),
            pltpu.VMEM((2, 2 * lat, lev), jnp.float32),
            pltpu.VMEM((2, 2 * lat, lev), jnp.float32),
            pltpu.VMEM((2 * lat, width // 2), jnp.float32),
            pltpu.VMEM(lit.shape, lit.dtype),
            pltpu.VMEM((width // 2, 128), jnp.float32),
            pltpu.VMEM(w_in.shape, w_in.dtype),
            pltpu.VMEM(w_a.shape, w_a.dtype),
            pltpu.VMEM(w_b.shape, w_b.dtype),
            pltpu.VMEM(w_out.shape, w_out.dtype),
            pltpu.SemaphoreType.DMA((steps,)),
            pltpu.SemaphoreType.DMA((7,)),
            pltpu.SemaphoreType.DMA((2,)),
            pltpu.SemaphoreType.DMA((2,)),
            pltpu.SemaphoreType.DMA((2,)),
        ],
        compiler_params=pltpu.CompilerParams(
            vmem_limit_bytes=KERNEL_MIB * 1024 * 1024, collective_id=0, has_side_effects=True
        ),
        cost_estimate=pl.CostEstimate(
            flops=lat * width * 720896, bytes_accessed=10 * 1024 * 1024,
            transcendentals=lat * width // 2 * 1536,
        ),
        name="column_step",
    )(x, lit, lon, lat_push, w_in, w_a, w_b, w_out)


def shards(column_state, daylit, courant_lon, courant_lat, w_in, w_mid_a, w_mid_b, w_out):
    _, lat, cols, fields, lev = column_state.shape
    out = column_step(
        column_state.reshape(lat, cols * fields, lev), daylit[0], courant_lon[0], courant_lat[0],
        w_in, w_mid_a, w_mid_b, w_out, 4
    )
    return out.reshape(column_state.shape)


def solution(mesh):
    placed = (
        P("groups", None, "lon", None, None),
        P("groups", None, "lon"),
        P("groups", None, "lon"),
        P("groups", None, "lon"),
        P(),
        P(),
        P(),
        P(),
    )
    return jax.shard_map(
        shards,
        mesh=mesh,
        in_specs=placed,
        out_specs=P("groups", None, "lon", None, None),
        check_vma=False,
    )
```
